32 devices in a mesh: tm: 4 (over y, x), pix: 8 (over z, core).
Axes of the slice: x: 2, y: 2, z: 4, core: 2. Of those that a mesh axis runs over, the one named last changes fastest.
Arguments:
- latent: float32 [16, 32, 448], P(None, 'pix'), may hold values from -6 to 6
- step_size: float32 [8], P('tm'), may hold values from 0.05 to 0.2
- time_embed: float32 [8, 128], P('tm'), may hold values from -6 to 6
- conv_in: bfloat16 [3, 3, 128, 16], replicated, may hold values from -0.5 to 0.5
- conv_mid: bfloat16 [3, 3, 128, 128], replicated, may hold values from -0.1875 to 0.1875
- conv_out: bfloat16 [3, 3, 16, 128], replicated, may hold values from -0.1875 to 0.1875
Outputs:
- trajectory: float32 [8, 16, 32, 448], P('tm', None, 'pix')
The draws below stay inside these ranges and needn't reach their ends.
All inputs are finite; a program needn't handle non-finite values.
Results may differ from the reference program's by a relative error of at most 0.00075.
Values may be sent and summed in bfloat16 or wider, within the bound.
A program may use at most 64 MiB of HBM per device.

```python
import math
import jax
import jax.numpy as jnp
from jax import lax

C = 16
F = 128
W = 448
ITERS = 3
H = 32
TIMES = 8


def level_of(stream_key, extent, split, low, top_value):
    factor_of, own = 1.0, jax.random.fold_in(stream_key, 6)
    for dim, shards_of in split:
        draws = jnp.exp(jax.random.uniform(jax.random.fold_in(own, dim), (shards_of,), jnp.float32, low / len(split), top_value / len(split)))
        factor_of = factor_of * jnp.repeat(draws, extent[dim] // shards_of).reshape([-1 if axis == dim else 1 for axis in range(len(extent))])
    return factor_of


def scatter_about(rng, shape, deviation, limit, shards=(), kind=jnp.bfloat16):
    gain = level_of(rng, shape, shards, -0.22, 0.18) if shards else 1.0
    entries = jax.random.normal(rng, shape, jnp.float32) * deviation * gain
    return jnp.minimum(jnp.maximum(entries, -limit), limit).astype(kind)


def setup_inputs(seed: int = 0) -> dict:
    arg_keys = jax.random.split(jax.random.key(seed), 7)
    latent = scatter_about(arg_keys[0], (C, H, W), 1.0, 6.0, ((1, 8),), jnp.float32)
    step_size = jnp.clip(jnp.exp(math.log(0.2) - 1.3862944 * jax.random.uniform(arg_keys[1], (TIMES,), jnp.float32) ** level_of(arg_keys[1], (TIMES,), ((0, 4),), -0.2, 0.2)), 0.05, 0.2)
    time_embed = scatter_about(arg_keys[2], (TIMES, F), 1.0, 6.0, ((0, 4),), jnp.float32)
    conv_in = scatter_about(arg_keys[3], (3, 3, F, C), (9 * C) ** -0.5, 0.5)
    conv_mid = scatter_about(arg_keys[4], (3, 3, F, F), (9 * F) ** -0.5, 0.1875)
    conv_out = scatter_about(arg_keys[5], (3, 3, C, F), (9 * F) ** -0.5, 0.1875)
    return {"latent": latent, "step_size": step_size, "time_embed": time_embed, "conv_in": conv_in, "conv_mid": conv_mid, "conv_out": conv_out}


def convolve(values, kernel):
    height = values.shape[1]
    span_cols = values.shape[2]
    padded = jnp.pad(values.astype(jnp.float32), ((0, 0), (1, 1), (1, 1)))
    summed = jnp.zeros((kernel.shape[2], height, span_cols), jnp.float32)
    for row_shift in range(3):
        for col_shift in range(3):
            summed = summed + jnp.einsum("oi,ihw->ohw", kernel[row_shift, col_shift].astype(jnp.float32), padded[:, row_shift:row_shift + height, col_shift:col_shift + span_cols])
    return summed


def reference(latent, step_size, time_embed, conv_in, conv_mid, conv_out):
    def denoise(inputs):
        current, time_vec = inputs
        first_pre = convolve(current.astype(jnp.bfloat16), conv_in) + time_vec[:, None, None]
        hidden = jax.nn.silu(first_pre).astype(jnp.bfloat16)
        second = jax.nn.silu(convolve(hidden, conv_mid)).astype(jnp.bfloat16)
        return current + convolve(second, conv_out)

    states = jnp.broadcast_to(latent[None], (TIMES,) + latent.shape)
    trajectory = states
    for rounds in range(ITERS):
        outputs = lax.map(denoise, (states, time_embed))
        drifts = step_size[:, None, None, None] * outputs
        trajectory = latent[None] + jnp.cumsum(drifts, axis=0)
        states = jnp.concatenate([latent[None], trajectory[:-1]], axis=0)
    return trajectory
```

```python
import functools

import jax
import jax.numpy as jnp
from jax import lax
from jax.experimental import pallas as pl
from jax.experimental.pallas import tpu as pltpu
from jax.sharding import PartitionSpec as P

ITERS = 3
LANES = 128
MESH = pl.DeviceIdType.MESH


def kernel(
    sizes,
    step_ref, latent_ref, te_ref, cin_ref, cmid_ref, cout_ref,
    out_ref,
    win, wmid, wout, lat, low0, halo0, im, pre0, hid, ysum, mask,
    table, bias, own, stage, halo, final, landed,
    sem0_send, sem0_recv, tab_send, tab_recv, halo_send, halo_recv, fin_send, fin_recv,
):
    sections, peers, per, total, chan, feat, rows, width, cols, margin, lanes = sizes
    q, p = lax.axis_index("tm"), lax.axis_index("pix")
    evals = total - ITERS + 1
    edge = 3 * lanes
    hid_rows, sec_rows, low_rows = rows + 4, rows + 2, rows + 6

    barrier = pltpu.get_barrier_semaphore()
    for s in range(1, sections):
        pl.semaphore_signal(barrier, inc=1, device_id=(lax.rem(q + s, sections), p), device_id_type=MESH)

    @pl.when(p > 0)
    def _():
        pl.semaphore_signal(barrier, inc=1, device_id=(q, p - 1), device_id_type=MESH)

    @pl.when(p < peers - 1)
    def _():
        pl.semaphore_signal(barrier, inc=1, device_id=(q, p + 1), device_id_type=MESH)

    for j in range(per):
        table[q * per + j] = jnp.concatenate(
            [te_ref[j : j + 1, :], jnp.full((7, feat), step_ref[j], jnp.float32)], axis=0
        )

    padded = (width + 2 * margin + LANES - 1) // LANES * LANES
    for r in range(rows):
        line = jnp.concatenate(
            [latent_ref[:, r, :], jnp.zeros((chan, padded - width), jnp.float32)], axis=1
        )
        for b in range(3):
            shift = lax.rem(margin + 1 - b - q * cols + 2 * padded, padded)
            view = pltpu.roll(line, shift, 1)[:, :lanes]
            low0[b, :, r * lanes : (r + 1) * lanes] = view.astype(jnp.bfloat16)
            if b == 1:
                lat[:, r * lanes : (r + 1) * lanes] = view

    @pl.when(p == 0)
    def _():
        halo0[0] = jnp.zeros(halo0.shape[1:], jnp.bfloat16)
        halo[0] = jnp.zeros(halo.shape[1:], jnp.bfloat16)

    @pl.when(p == peers - 1)
    def _():
        halo0[1] = jnp.zeros(halo0.shape[1:], jnp.bfloat16)
        halo[1] = jnp.zeros(halo.shape[1:], jnp.bfloat16)

    def table_copy(s):
        mine = table.at[pl.ds(q * per, per)]
        return pltpu.make_async_remote_copy(
            src_ref=mine, dst_ref=mine, send_sem=tab_send.at[s - 1], recv_sem=tab_recv.at[s - 1],
            device_id=(lax.rem(q + s, sections), p), device_id_type=MESH,
        )

    def first_copy(up):
        src = low0.at[:, :, pl.ds(0 if up else (rows - 3) * lanes, edge)]
        return pltpu.make_async_remote_copy(
            src_ref=src, dst_ref=halo0.at[1 if up else 0],
            send_sem=sem0_send.at[1 if up else 0], recv_sem=sem0_recv.at[1 if up else 0],
            device_id=(q, p - 1 if up else p + 1), device_id_type=MESH,
        )

    def halo_copy(up, slot):
        src = stage.at[slot, :, pl.ds(0 if up else (rows - 3) * lanes, edge)]
        side = 1 if up else 0
        return pltpu.make_async_remote_copy(
            src_ref=src, dst_ref=halo.at[side, slot],
            send_sem=halo_send.at[side, slot], recv_sem=halo_recv.at[side, slot],
            device_id=(q, p - 1 if up else p + 1), device_id_type=MESH,
        )

    def final_copy(source, j):
        return pltpu.make_async_remote_copy(
            src_ref=source, dst_ref=landed.at[q, lax.rem(j, per)],
            send_sem=fin_send.at[j], recv_sem=fin_recv.at[q, lax.rem(j, per)],
            device_id=(lax.div(j, per), p), device_id_type=MESH,
        )

    def deliver(source, j):
        owner = lax.div(jnp.int32(j), jnp.int32(per))

        @pl.when(owner == q)
        def _():
            landed[q, lax.rem(j, per)] = source[...]

        @pl.when(owner != q)
        def _():
            final_copy(source, j).start()

    pl.semaphore_wait(
        barrier, sections - 1 + (p > 0).astype(jnp.int32) + (p < peers - 1).astype(jnp.int32)
    )

    @pl.when(p > 0)
    def _():
        first_copy(True).start()

    @pl.when(p < peers - 1)
    def _():
        first_copy(False).start()

    for s in range(1, sections):
        table_copy(s).start()

    for a in range(3):
        for b in range(3):
            t = 3 * a + b
            win[:, t * chan : (t + 1) * chan] = cin_ref[a, b]
            wmid[:, t * feat : (t + 1) * feat] = cmid_ref[a, b]
            wout[t * chan : (t + 1) * chan, :] = cout_ref[a, b]

    col = lax.broadcasted_iota(jnp.int32, (8, lanes), 1) + (q * cols - margin)
    inside = jnp.where((col >= 0) & (col < width), 0.5, 0.0).astype(jnp.float32)
    for h in range(hid_rows):
        row = p * rows - 2 + h
        valid = ((row >= 0) & (row < peers * rows)).astype(jnp.float32)
        mask[:, h * lanes : (h + 1) * lanes] = inside * valid

    def gated(v, m):
        h = v * m
        return h + h * jnp.tanh(h)

    def spread(lows):
        for a in range(3):
            for b in range(3):
                t = 3 * a + b
                im[t * chan : (t + 1) * chan, :] = lows[b][:, a * lanes : (a + hid_rows) * lanes]

    def first_layer(pre, j, h0, count):
        te = bias[j]
        for i in range(count):
            h = h0 + i
            v = pre[:, i * lanes : (i + 1) * lanes] + te
            x = gated(v, mask[0:1, h * lanes : (h + 1) * lanes])
            span = slice(h * lanes, (h + 1) * lanes)
            hid[0:feat, span] = pltpu.roll(x, 1, 1).astype(jnp.bfloat16)
            hid[feat : 2 * feat, span] = x.astype(jnp.bfloat16)
            hid[2 * feat :, span] = pltpu.roll(x, lanes - 1, 1).astype(jnp.bfloat16)

    def rest(j):
        w = wmid[...]
        for s0 in range(0, sec_rows, 2):
            n = min(2, sec_rows - s0)
            x = jnp.concatenate(
                [hid[:, (s0 + a) * lanes : (s0 + a + n) * lanes] for a in range(3)], axis=0
            )
            v = jnp.dot(w, x, preferred_element_type=jnp.float32)
            m = mask[0:1, (s0 + 1) * lanes : (s0 + 1 + n) * lanes]
            second = gated(v, m).astype(jnp.bfloat16)
            ysum[:, s0 * lanes : (s0 + n) * lanes] = jnp.dot(
                wout[...], second, preferred_element_type=jnp.float32
            )
        parts = []
        for b in range(3):
            z = None
            for a in range(3):
                t = 3 * a + b
                y = ysum[t * chan : (t + 1) * chan, a * lanes : (a + rows) * lanes]
                z = y if z is None else z + y
            parts.append(z)
        return parts[1] + pltpu.roll(parts[0], 1, 1) + pltpu.roll(parts[2], rows * lanes - 1, 1)

    @pl.when(p < peers - 1)
    def _():
        first_copy(True).wait_recv()

    @pl.when(p > 0)
    def _():
        first_copy(False).wait_recv()

    spread([jnp.concatenate([halo0[0, b], low0[b], halo0[1, b]], axis=1) for b in range(3)])
    for h0 in range(0, hid_rows, 2):
        n = min(2, hid_rows - h0)
        span = slice(h0 * lanes, (h0 + n) * lanes)
        pre0[:, span] = jnp.dot(win[...], im[:, span], preferred_element_type=jnp.float32)

    for s in range(1, sections):
        table_copy(s).wait_recv()
    for j in range(total):
        bias[j] = jnp.broadcast_to(table[j, 0:1, :], (feat, feat)).T

    flat = jnp.concatenate([inside[0:1, :] * 2.0] * rows, axis=1)

    def advance(k, j, summed):
        slot = k * evals + j - k
        if k == 0:
            state = lat[...]
            first_layer(pre0[...], j, 0, hid_rows)
        else:
            came = slot - evals

            @pl.when(p < peers - 1)
            def _():
                halo_copy(True, came).wait_recv()

            @pl.when(p > 0)
            def _():
                halo_copy(False, came).wait_recv()

            state = own[came]
            centre = jnp.concatenate(
                [halo[0, came].astype(jnp.float32), state, halo[1, came].astype(jnp.float32)], axis=1
            )
            span = low_rows * lanes
            spread([
                pltpu.roll(centre, 1, 1).astype(jnp.bfloat16),
                centre.astype(jnp.bfloat16),
                pltpu.roll(centre, span - 1, 1).astype(jnp.bfloat16),
            ])
            for h0 in range(0, hid_rows, 2):
                n = min(2, hid_rows - h0)
                pre = jnp.dot(
                    win[...], im[:, h0 * lanes : (h0 + n) * lanes], preferred_element_type=jnp.float32
                )
                first_layer(pre, j, h0, n)
        output = state + rest(j)
        step = table[j, 1:2, :]
        summed = summed + jnp.concatenate([step] * rows, axis=1) * output
        reached = lat[...] + summed
        if k < ITERS - 1:
            reached = reached * flat
            own[slot] = reached
            stage[slot] = reached.astype(jnp.bfloat16)

            @pl.when(p > 0)
            def _():
                halo_copy(True, slot).start()

            @pl.when(p < peers - 1)
            def _():
                halo_copy(False, slot).start()
        else:
            final[j] = reached
            deliver(final.at[j], j)
        return summed

    start = jnp.zeros((chan, rows * lanes), jnp.float32)
    for k in range(ITERS):
        first = advance(k, jnp.int32(k), start)
        if k < ITERS - 1:
            deliver(own.at[k * evals], k)

        def body(j, summed, k=k):
            return advance(k, j, summed)

        lax.fori_loop(k + 1, k + evals, body, first)
        start = first

    for s in range(1, sections):
        table_copy(s).wait_send()

    @pl.when(p > 0)
    def _():
        first_copy(True).wait_send()

    @pl.when(p < peers - 1)
    def _():
        first_copy(False).wait_send()

    def drain(slot, carry):
        @pl.when(p > 0)
        def _():
            halo_copy(True, slot).wait_send()

        @pl.when(p < peers - 1)
        def _():
            halo_copy(False, slot).wait_send()

        return carry

    lax.fori_loop(0, (ITERS - 1) * evals, drain, 0)

    for j in range(total):
        @pl.when(jnp.int32(j // per) != q)
        def _(j=j):
            final_copy(final.at[j], jnp.int32(j)).wait_send()

    for s in range(sections):
        @pl.when(q != s)
        def _(s=s):
            for j in range(per):
                pltpu.make_async_remote_copy(
                    src_ref=landed.at[s, j], dst_ref=landed.at[s, j],
                    send_sem=fin_send.at[j], recv_sem=fin_recv.at[s, j],
                    device_id=(jnp.int32(s), p), device_id_type=MESH,
                ).wait_recv()

    for s in range(sections):
        for j in range(per):
            block = landed[s, j]
            for r in range(rows):
                out_ref[j, r, :, s * cols : (s + 1) * cols] = block[
                    :, r * lanes + margin : r * lanes + margin + cols
                ]


def shards(latent, step_size, time_embed, conv_in, conv_mid, conv_out):
    sections, peers = lax.axis_size("tm"), lax.axis_size("pix")
    chan, rows, width = latent.shape
    per, feat = time_embed.shape
    total = sections * per
    cols = width // sections
    margin = 3 * ITERS - 1
    lanes = (cols + 2 * margin + LANES - 1) // LANES * LANES
    evals = total - ITERS + 1
    slots = (ITERS - 1) * evals
    sizes = (sections, peers, per, total, chan, feat, rows, width, cols, margin, lanes)
    vmem = pl.BlockSpec(memory_space=pltpu.VMEM)
    f32, bf16 = jnp.float32, jnp.bfloat16
    dma = pltpu.SemaphoreType.DMA
    out = pl.pallas_call(
        functools.partial(kernel, sizes),
        out_shape=jax.ShapeDtypeStruct((per, rows, chan, width), f32),
        in_specs=[pl.BlockSpec(memory_space=pltpu.SMEM)] + [vmem] * 5,
        out_specs=vmem,
        scratch_shapes=[
            pltpu.VMEM((feat, 9 * chan), bf16),
            pltpu.VMEM((feat, 9 * feat), bf16),
            pltpu.VMEM((9 * chan, feat), bf16),
            pltpu.VMEM((chan, rows * lanes), f32),
            pltpu.VMEM((3, chan, rows * lanes), bf16),
            pltpu.VMEM((2, 3, chan, 3 * lanes), bf16),
            pltpu.VMEM((9 * chan, (rows + 4) * lanes), bf16),
            pltpu.VMEM((feat, (rows + 4) * lanes), f32),
            pltpu.VMEM((3 * feat, (rows + 4) * lanes), bf16),
            pltpu.VMEM((9 * chan, (rows + 2) * lanes), f32),
            pltpu.VMEM((8, (rows + 4) * lanes), f32),
            pltpu.VMEM((total, 8, feat), f32),
            pltpu.VMEM((total, feat, feat), f32),
            pltpu.VMEM((slots, chan, rows * lanes), f32),
            pltpu.VMEM((slots, chan, rows * lanes), bf16),
            pltpu.VMEM((2, slots, chan, 3 * lanes), bf16),
            pltpu.VMEM((total, chan, rows * lanes), f32),
            pltpu.VMEM((sections, per, chan, rows * lanes), f32),
            dma((2,)), dma((2,)),
            dma((sections - 1,)), dma((sections - 1,)),
            dma((2, slots)), dma((2, slots)),
            dma((total,)), dma((sections, per)),
        ],
        compiler_params=pltpu.CompilerParams(
            collective_id=0, has_side_effects=True, vmem_limit_bytes=40 * 1024 * 1024
        ),
    )(step_size, latent, time_embed, conv_in, conv_mid, conv_out)
    return jnp.transpose(out, (0, 2, 1, 3))


def solution(mesh):
    in_specs = (P(None, "pix", None), P("tm"), P("tm", None), P(), P(), P())
    out_specs = P("tm", None, "pix", None)
    return jax.shard_map(shards, mesh=mesh, in_specs=in_specs, out_specs=out_specs, check_vma=False)
```

```python
import functools

import jax
import jax.numpy as jnp
from jax import lax
from jax.experimental import pallas as pl
from jax.experimental.pallas import tpu as pltpu
from jax.sharding import PartitionSpec as P

ITERS = 3
GROUP = 3
LANES = 128
MESH = pl.DeviceIdType.MESH


def kernel(
    sizes,
    step_ref, latent_ref, te_ref, cin_ref, cmid_ref, cout_ref,
    out_ref,
    win, wmid, wout, lat, low0, halo0, im, pre0, hid, ysum, mask,
    table, bias, own, stage, halo, final, landed, start,
    sem0_send, sem0_recv, tab_send, tab_recv, halo_send, halo_recv, fin_send, fin_recv,
):
    sections, peers, per, total, chan, feat, rows, width, cols, margin, lanes, group = sizes
    q, p = lax.axis_index("tm"), lax.axis_index("pix")
    evals = total - ITERS + 1
    edge = 3 * lanes
    hid_rows, sec_rows, low_rows = rows + 4, rows + 2, rows + 6

    barrier = pltpu.get_barrier_semaphore()
    for s in range(1, sections):
        pl.semaphore_signal(barrier, inc=1, device_id=(lax.rem(q + s, sections), p), device_id_type=MESH)

    @pl.when(p > 0)
    def _():
        pl.semaphore_signal(barrier, inc=1, device_id=(q, p - 1), device_id_type=MESH)

    @pl.when(p < peers - 1)
    def _():
        pl.semaphore_signal(barrier, inc=1, device_id=(q, p + 1), device_id_type=MESH)

    for j in range(per):
        table[q * per + j] = jnp.concatenate(
            [te_ref[j : j + 1, :], jnp.full((7, feat), step_ref[j], jnp.float32)], axis=0
        )

    padded = (width + 2 * margin + LANES - 1) // LANES * LANES
    for r in range(rows):
        line = jnp.concatenate(
            [latent_ref[:, r, :], jnp.zeros((chan, padded - width), jnp.float32)], axis=1
        )
        for b in range(3):
            shift = lax.rem(margin + 1 - b - q * cols + 2 * padded, padded)
            view = pltpu.roll(line, shift, 1)[:, :lanes]
            low0[b, :, r * lanes : (r + 1) * lanes] = view.astype(jnp.bfloat16)
            if b == 1:
                lat[:, r * lanes : (r + 1) * lanes] = view

    @pl.when(p == 0)
    def _():
        halo0[0] = jnp.zeros(halo0.shape[1:], jnp.bfloat16)
        halo[0] = jnp.zeros(halo.shape[1:], jnp.bfloat16)

    @pl.when(p == peers - 1)
    def _():
        halo0[1] = jnp.zeros(halo0.shape[1:], jnp.bfloat16)
        halo[1] = jnp.zeros(halo.shape[1:], jnp.bfloat16)

    def table_copy(s):
        mine = table.at[pl.ds(q * per, per)]
        return pltpu.make_async_remote_copy(
            src_ref=mine, dst_ref=mine, send_sem=tab_send.at[s - 1], recv_sem=tab_recv.at[s - 1],
            device_id=(lax.rem(q + s, sections), p), device_id_type=MESH,
        )

    def first_copy(up):
        src = low0.at[:, :, pl.ds(0 if up else (rows - 3) * lanes, edge)]
        return pltpu.make_async_remote_copy(
            src_ref=src, dst_ref=halo0.at[1 if up else 0],
            send_sem=sem0_send.at[1 if up else 0], recv_sem=sem0_recv.at[1 if up else 0],
            device_id=(q, p - 1 if up else p + 1), device_id_type=MESH,
        )

    def halo_copy(up, slot):
        src = stage.at[slot, :, pl.ds(0 if up else (rows - 3) * lanes, edge)]
        side = 1 if up else 0
        return pltpu.make_async_remote_copy(
            src_ref=src, dst_ref=halo.at[side, slot],
            send_sem=halo_send.at[side, slot], recv_sem=halo_recv.at[side, slot],
            device_id=(q, p - 1 if up else p + 1), device_id_type=MESH,
        )

    def final_copy(source, j):
        return pltpu.make_async_remote_copy(
            src_ref=source, dst_ref=landed.at[q, lax.rem(j, per)],
            send_sem=fin_send.at[j], recv_sem=fin_recv.at[q, lax.rem(j, per)],
            device_id=(lax.div(j, per), p), device_id_type=MESH,
        )

    def deliver(source, j):
        owner = lax.div(jnp.int32(j), jnp.int32(per))

        @pl.when(owner == q)
        def _():
            landed[q, lax.rem(j, per)] = source[...]

        @pl.when(owner != q)
        def _():
            final_copy(source, j).start()

    pl.semaphore_wait(
        barrier, sections - 1 + (p > 0).astype(jnp.int32) + (p < peers - 1).astype(jnp.int32)
    )

    @pl.when(p > 0)
    def _():
        first_copy(True).start()

    @pl.when(p < peers - 1)
    def _():
        first_copy(False).start()

    for s in range(1, sections):
        table_copy(s).start()

    for a in range(3):
        for b in range(3):
            t = 3 * a + b
            wmid[:, t * feat : (t + 1) * feat] = cmid_ref[a, b]
            wout[t * chan : (t + 1) * chan, :] = cout_ref[a, b]

    taps = jnp.concatenate([cin_ref[t // 3, t % 3] for t in range(9)], axis=0)
    win[...] = taps.astype(jnp.float32).T.astype(jnp.bfloat16)

    col = lax.broadcasted_iota(jnp.int32, (8, lanes), 1) + (q * cols - margin)
    inside = jnp.where((col >= 0) & (col < width), 0.5, 0.0).astype(jnp.float32)
    for h in range(hid_rows):
        row = p * rows - 2 + h
        valid = ((row >= 0) & (row < peers * rows)).astype(jnp.float32)
        mask[:, h * lanes : (h + 1) * lanes] = inside * valid

    def gated(v, m):
        h = v * m
        return h + h * jnp.tanh(h)

    def spread(u, lows):
        for a in range(3):
            for b in range(3):
                t = 3 * a + b
                im[u, t * chan : (t + 1) * chan, :] = lows[b][:, a * lanes : (a + hid_rows) * lanes]

    def first_layer(u, pre, j, h0, count):
        te = bias[j]
        for i in range(count):
            h = h0 + i
            v = pre[:, i * lanes : (i + 1) * lanes] + te
            x = gated(v, mask[0:1, h * lanes : (h + 1) * lanes])
            span = slice(h * lanes, (h + 1) * lanes)
            hid[u, 0:feat, span] = pltpu.roll(x, 1, 1).astype(jnp.bfloat16)
            hid[u, feat : 2 * feat, span] = x.astype(jnp.bfloat16)
            hid[u, 2 * feat :, span] = pltpu.roll(x, lanes - 1, 1).astype(jnp.bfloat16)

    def second_layer(u, s0, n):
        x = jnp.concatenate(
            [hid[u, :, (s0 + a) * lanes : (s0 + a + n) * lanes] for a in range(3)], axis=0
        )
        v = jnp.dot(wmid[...], x, preferred_element_type=jnp.float32)
        return gated(v, mask[0:1, (s0 + 1) * lanes : (s0 + 1 + n) * lanes]).astype(jnp.bfloat16)

    def last_layer(u):
        parts = []
        for b in range(3):
            z = None
            for a in range(3):
                t = 3 * a + b
                y = ysum[u, t * chan : (t + 1) * chan, a * lanes : (a + rows) * lanes]
                z = y if z is None else z + y
            parts.append(z)
        return parts[1] + pltpu.roll(parts[0], 1, 1) + pltpu.roll(parts[2], rows * lanes - 1, 1)

    @pl.when(p < peers - 1)
    def _():
        first_copy(True).wait_recv()

    @pl.when(p > 0)
    def _():
        first_copy(False).wait_recv()

    spread(0, [jnp.concatenate([halo0[0, b], low0[b], halo0[1, b]], axis=1) for b in range(3)])
    for h0 in range(0, hid_rows, 2):
        n = min(2, hid_rows - h0)
        span = slice(h0 * lanes, (h0 + n) * lanes)
        pre0[:, span] = jnp.dot(win[...], im[0, :, span], preferred_element_type=jnp.float32)

    for s in range(1, sections):
        table_copy(s).wait_recv()
    for j in range(total):
        bias[j] = jnp.broadcast_to(table[j, 0:1, :], (lanes, feat)).T

    flat = jnp.concatenate([inside[0:1, :] * 2.0] * rows, axis=1)

    def advance(k, j0, summed):
        slots = [k * evals + j0 + u - k for u in range(group)]
        times = [j0 + u for u in range(group)]
        if k:
            @pl.when(p < peers - 1)
            def _():
                for slot in slots:
                    halo_copy(True, slot - evals).wait_recv()

            @pl.when(p > 0)
            def _():
                for slot in slots:
                    halo_copy(False, slot - evals).wait_recv()

            for u, slot in enumerate(slots):
                came = slot - evals
                centre = jnp.concatenate(
                    [halo[0, came].astype(jnp.float32), own[came], halo[1, came].astype(jnp.float32)],
                    axis=1,
                )
                spread(u, [
                    pltpu.roll(centre, 1, 1).astype(jnp.bfloat16),
                    centre.astype(jnp.bfloat16),
                    pltpu.roll(centre, low_rows * lanes - 1, 1).astype(jnp.bfloat16),
                ])
        for h0 in range(0, hid_rows, 2):
            n = min(2, hid_rows - h0)
            span = slice(h0 * lanes, (h0 + n) * lanes)
            for u in range(group):
                if k:
                    pre = jnp.dot(win[...], im[u, :, span], preferred_element_type=jnp.float32)
                else:
                    pre = pre0[:, span]
                first_layer(u, pre, times[u], h0, n)
        for s0 in range(0, sec_rows, 2):
            n = min(2, sec_rows - s0)
            seconds = [second_layer(u, s0, n) for u in range(group)]
            for u in range(group):
                ysum[u, :, s0 * lanes : (s0 + n) * lanes] = jnp.dot(
                    wout[...], seconds[u], preferred_element_type=jnp.float32
                )
        for u in range(group):
            state = own[slots[u] - evals] if k else lat[...]
            step = table[times[u], 1:2, :]
            summed = summed + jnp.concatenate([step] * rows, axis=1) * (state + last_layer(u))
            reached = lat[...] + summed
            if k < ITERS - 1:
                reached = reached * flat
                own[slots[u]] = reached
                stage[slots[u]] = reached.astype(jnp.bfloat16)
                if u == 0:
                    @pl.when(j0 == k)
                    def _(summed=summed):
                        start[...] = summed
            else:
                final[times[u]] = reached
        if k < ITERS - 1:
            @pl.when(p > 0)
            def _():
                for slot in slots:
                    halo_copy(True, slot).start()

            @pl.when(p < peers - 1)
            def _():
                for slot in slots:
                    halo_copy(False, slot).start()
        else:
            for j in times:
                deliver(final.at[j], j)
        return summed

    start[...] = jnp.zeros_like(start)
    for k in range(ITERS):

        def body(i, summed, k=k):
            return advance(k, k + i * group, summed)

        lax.fori_loop(0, evals // group, body, start[...])
        if k < ITERS - 1:
            deliver(own.at[k * evals], jnp.int32(k))

    for s in range(1, sections):
        table_copy(s).wait_send()

    @pl.when(p > 0)
    def _():
        first_copy(True).wait_send()

    @pl.when(p < peers - 1)
    def _():
        first_copy(False).wait_send()

    def drain(slot, carry):
        @pl.when(p > 0)
        def _():
            halo_copy(True, slot).wait_send()

        @pl.when(p < peers - 1)
        def _():
            halo_copy(False, slot).wait_send()

        return carry

    lax.fori_loop(0, (ITERS - 1) * evals, drain, 0)

    for j in range(total):
        @pl.when(jnp.int32(j // per) != q)
        def _(j=j):
            final_copy(final.at[j], jnp.int32(j)).wait_send()

    for s in range(sections):
        @pl.when(q != s)
        def _(s=s):
            for j in range(per):
                pltpu.make_async_remote_copy(
                    src_ref=landed.at[s, j], dst_ref=landed.at[s, j],
                    send_sem=fin_send.at[j], recv_sem=fin_recv.at[s, j],
                    device_id=(jnp.int32(s), p), device_id_type=MESH,
                ).wait_recv()

    for s in range(sections):
        for j in range(per):
            block = landed[s, j]
            for r in range(rows):
                out_ref[j, r, :, s * cols : (s + 1) * cols] = block[
                    :, r * lanes + margin : r * lanes + margin + cols
                ]


def shards(latent, step_size, time_embed, conv_in, conv_mid, conv_out):
    sections, peers = lax.axis_size("tm"), lax.axis_size("pix")
    chan, rows, width = latent.shape
    per, feat = time_embed.shape
    total = sections * per
    cols = width // sections
    margin = 3 * ITERS - 1
    lanes = (cols + 2 * margin + LANES - 1) // LANES * LANES
    evals = total - ITERS + 1
    slots = (ITERS - 1) * evals
    group = next(g for g in (GROUP, 2, 1) if evals % g == 0)
    sizes = (sections, peers, per, total, chan, feat, rows, width, cols, margin, lanes, group)
    vmem = pl.BlockSpec(memory_space=pltpu.VMEM)
    f32, bf16 = jnp.float32, jnp.bfloat16
    dma = pltpu.SemaphoreType.DMA
    out = pl.pallas_call(
        functools.partial(kernel, sizes),
        out_shape=jax.ShapeDtypeStruct((per, rows, chan, width), f32),
        in_specs=[pl.BlockSpec(memory_space=pltpu.SMEM)] + [vmem] * 5,
        out_specs=vmem,
        scratch_shapes=[
            pltpu.VMEM((feat, 9 * chan), bf16),
            pltpu.VMEM((feat, 9 * feat), bf16),
            pltpu.VMEM((9 * chan, feat), bf16),
            pltpu.VMEM((chan, rows * lanes), f32),
            pltpu.VMEM((3, chan, rows * lanes), bf16),
            pltpu.VMEM((2, 3, chan, 3 * lanes), bf16),
            pltpu.VMEM((group, 9 * chan, (rows + 4) * lanes), bf16),
            pltpu.VMEM((feat, (rows + 4) * lanes), f32),
            pltpu.VMEM((group, 3 * feat, (rows + 4) * lanes), bf16),
            pltpu.VMEM((group, 9 * chan, (rows + 2) * lanes), f32),
            pltpu.VMEM((8, (rows + 4) * lanes), f32),
            pltpu.VMEM((total, 8, feat), f32),
            pltpu.VMEM((total, feat, lanes), f32),
            pltpu.VMEM((slots, chan, rows * lanes), f32),
            pltpu.VMEM((slots, chan, rows * lanes), bf16),
            pltpu.VMEM((2, slots, chan, 3 * lanes), bf16),
            pltpu.VMEM((total, chan, rows * lanes), f32),
            pltpu.VMEM((sections, per, chan, rows * lanes), f32),
            pltpu.VMEM((chan, rows * lanes), f32),
            dma((2,)), dma((2,)),
            dma((sections - 1,)), dma((sections - 1,)),
            dma((2, slots)), dma((2, slots)),
            dma((total,)), dma((sections, per)),
        ],
        compiler_params=pltpu.CompilerParams(
            collective_id=0, has_side_effects=True, vmem_limit_bytes=40 * 1024 * 1024
        ),
    )(step_size, latent, time_embed, jnp.swapaxes(conv_in, 2, 3), conv_mid, conv_out)
    return jnp.transpose(out, (0, 2, 1, 3))


def solution(mesh):
    in_specs = (P(None, "pix", None), P("tm"), P("tm", None), P(), P(), P())
    out_specs = P("tm", None, "pix", None)
    return jax.shard_map(shards, mesh=mesh, in_specs=in_specs, out_specs=out_specs, check_vma=False)
```

```python
import functools

import jax
import jax.numpy as jnp
from jax import lax
from jax.experimental import pallas as pl
from jax.experimental.pallas import tpu as pltpu
from jax.sharding import PartitionSpec as P

ITERS = 3
GROUP = 3
LANES = 128
MESH = pl.DeviceIdType.MESH


def kernel(
    sizes,
    step_hbm, latent_hbm, te_hbm, cin_hbm, cmid_hbm, cout_hbm,
    out_ref,
    win, wmid, wout, lat, low0, halo0, im, pre0, hid, ysum, mask,
    table, bias, own, stage, halo, final, landed, start,
    step_ref, latent_ref, te_ref, cin_ref, cmid_ref, cout_ref, load_sem,
    sem0_send, sem0_recv, tab_send, tab_recv, halo_send, halo_recv, fin_send, fin_recv,
):
    sections, peers, per, total, chan, feat, rows, width, cols, margin, lanes, group = sizes
    q, p = lax.axis_index("tm"), lax.axis_index("pix")
    evals = total - ITERS + 1
    edge = 3 * lanes
    hid_rows, sec_rows, low_rows = rows + 4, rows + 2, rows + 6

    loads = [
        pltpu.make_async_copy(source, target, load_sem.at[i])
        for i, (source, target) in enumerate([
            (latent_hbm, latent_ref), (te_hbm, te_ref), (step_hbm, step_ref),
            (cin_hbm, cin_ref), (cmid_hbm, cmid_ref), (cout_hbm, cout_ref),
        ])
    ]
    for load in loads:
        load.start()

    barrier = pltpu.get_barrier_semaphore()
    for s in range(1, sections):
        pl.semaphore_signal(barrier, inc=1, device_id=(lax.rem(q + s, sections), p), device_id_type=MESH)

    @pl.when(p > 0)
    def _():
        pl.semaphore_signal(barrier, inc=1, device_id=(q, p - 1), device_id_type=MESH)

    @pl.when(p < peers - 1)
    def _():
        pl.semaphore_signal(barrier, inc=1, device_id=(q, p + 1), device_id_type=MESH)

    for load in loads[:3]:
        load.wait()

    for j in range(per):
        table[q * per + j] = jnp.concatenate(
            [te_ref[j : j + 1, :], jnp.full((7, feat), step_ref[j], jnp.float32)], axis=0
        )

    padded = (width + 2 * margin + LANES - 1) // LANES * LANES
    for r in range(rows):
        line = jnp.concatenate(
            [latent_ref[:, r, :], jnp.zeros((chan, padded - width), jnp.float32)], axis=1
        )
        for b in range(3):
            shift = lax.rem(margin + 1 - b - q * cols + 2 * padded, padded)
            view = pltpu.roll(line, shift, 1)[:, :lanes]
            low0[b, :, r * lanes : (r + 1) * lanes] = view.astype(jnp.bfloat16)
            if b == 1:
                lat[:, r * lanes : (r + 1) * lanes] = view

    @pl.when(p == 0)
    def _():
        halo0[0] = jnp.zeros(halo0.shape[1:], jnp.bfloat16)
        halo[0] = jnp.zeros(halo.shape[1:], jnp.bfloat16)

    @pl.when(p == peers - 1)
    def _():
        halo0[1] = jnp.zeros(halo0.shape[1:], jnp.bfloat16)
        halo[1] = jnp.zeros(halo.shape[1:], jnp.bfloat16)

    def table_copy(s):
        mine = table.at[pl.ds(q * per, per)]
        return pltpu.make_async_remote_copy(
            src_ref=mine, dst_ref=mine, send_sem=tab_send.at[s - 1], recv_sem=tab_recv.at[s - 1],
            device_id=(lax.rem(q + s, sections), p), device_id_type=MESH,
        )

    def first_copy(up):
        src = low0.at[:, :, pl.ds(0 if up else (rows - 3) * lanes, edge)]
        return pltpu.make_async_remote_copy(
            src_ref=src, dst_ref=halo0.at[1 if up else 0],
            send_sem=sem0_send.at[1 if up else 0], recv_sem=sem0_recv.at[1 if up else 0],
            device_id=(q, p - 1 if up else p + 1), device_id_type=MESH,
        )

    def halo_copy(up, slot):
        src = stage.at[slot, :, pl.ds(0 if up else (rows - 3) * lanes, edge)]
        side = 1 if up else 0
        return pltpu.make_async_remote_copy(
            src_ref=src, dst_ref=halo.at[side, slot],
            send_sem=halo_send.at[side, slot], recv_sem=halo_recv.at[side, slot],
            device_id=(q, p - 1 if up else p + 1), device_id_type=MESH,
        )

    def final_copy(source, j):
        return pltpu.make_async_remote_copy(
            src_ref=source, dst_ref=landed.at[q, lax.rem(j, per)],
            send_sem=fin_send.at[j], recv_sem=fin_recv.at[q, lax.rem(j, per)],
            device_id=(lax.div(j, per), p), device_id_type=MESH,
        )

    def deliver(source, j):
        owner = lax.div(jnp.int32(j), jnp.int32(per))

        @pl.when(owner == q)
        def _():
            landed[q, lax.rem(j, per)] = source[...]

        @pl.when(owner != q)
        def _():
            final_copy(source, j).start()

    pl.semaphore_wait(
        barrier, sections - 1 + (p > 0).astype(jnp.int32) + (p < peers - 1).astype(jnp.int32)
    )

    @pl.when(p > 0)
    def _():
        first_copy(True).start()

    @pl.when(p < peers - 1)
    def _():
        first_copy(False).start()

    for s in range(1, sections):
        table_copy(s).start()

    for load in loads[3:]:
        load.wait()

    for a in range(3):
        for b in range(3):
            t = 3 * a + b
            wmid[:, t * feat : (t + 1) * feat] = cmid_ref[a, b]
            wout[t * chan : (t + 1) * chan, :] = cout_ref[a, b]

    taps = jnp.concatenate([cin_ref[t // 3, t % 3] for t in range(9)], axis=0)
    win[...] = taps.astype(jnp.float32).T.astype(jnp.bfloat16)

    col = lax.broadcasted_iota(jnp.int32, (8, lanes), 1) + (q * cols - margin)
    inside = jnp.where((col >= 0) & (col < width), 0.5, 0.0).astype(jnp.float32)
    for h in range(hid_rows):
        row = p * rows - 2 + h
        valid = ((row >= 0) & (row < peers * rows)).astype(jnp.float32)
        mask[:, h * lanes : (h + 1) * lanes] = inside * valid

    def gated(v, m):
        h = v * m
        return h + h * jnp.tanh(h)

    def spread(u, lows):
        for a in range(3):
            for b in range(3):
                t = 3 * a + b
                im[u, t * chan : (t + 1) * chan, :] = lows[b][:, a * lanes : (a + hid_rows) * lanes]

    def first_layer(u, pre, j, h0, count):
        te = bias[j]
        for i in range(count):
            h = h0 + i
            v = pre[:, i * lanes : (i + 1) * lanes] + te
            x = gated(v, mask[0:1, h * lanes : (h + 1) * lanes]).astype(jnp.bfloat16)
            span = slice(h * lanes, (h + 1) * lanes)
            hid[u, 0:feat, span] = pltpu.roll(x, 1, 1)
            hid[u, feat : 2 * feat, span] = x
            hid[u, 2 * feat :, span] = pltpu.roll(x, lanes - 1, 1)

    def second_layer(u, s0, n):
        x = jnp.concatenate(
            [hid[u, :, (s0 + a) * lanes : (s0 + a + n) * lanes] for a in range(3)], axis=0
        )
        v = jnp.dot(wmid[...], x, preferred_element_type=jnp.float32)
        return gated(v, mask[0:1, (s0 + 1) * lanes : (s0 + 1 + n) * lanes]).astype(jnp.bfloat16)

    def last_layer(u):
        parts = []
        for b in range(3):
            z = None
            for a in range(3):
                t = 3 * a + b
                y = ysum[u, t * chan : (t + 1) * chan, a * lanes : (a + rows) * lanes]
                z = y if z is None else z + y
            parts.append(z)
        return parts[1] + pltpu.roll(parts[0], 1, 1) + pltpu.roll(parts[2], rows * lanes - 1, 1)

    @pl.when(p < peers - 1)
    def _():
        first_copy(True).wait_recv()

    @pl.when(p > 0)
    def _():
        first_copy(False).wait_recv()

    spread(0, [jnp.concatenate([halo0[0, b], low0[b], halo0[1, b]], axis=1) for b in range(3)])
    for h0 in range(0, hid_rows, 2):
        n = min(2, hid_rows - h0)
        span = slice(h0 * lanes, (h0 + n) * lanes)
        pre0[:, span] = jnp.dot(win[...], im[0, :, span], preferred_element_type=jnp.float32)

    for s in range(1, sections):
        table_copy(s).wait_recv()
    for j in range(total):
        bias[j] = jnp.broadcast_to(table[j, 0:1, :], (lanes, feat)).T

    flat = jnp.concatenate([inside[0:1, :] * 2.0] * rows, axis=1)

    def advance(k, j0, summed):
        slots = [k * evals + j0 + u - k for u in range(group)]
        times = [j0 + u for u in range(group)]
        if k:
            @pl.when(p < peers - 1)
            def _():
                for slot in slots:
                    halo_copy(True, slot - evals).wait_recv()

            @pl.when(p > 0)
            def _():
                for slot in slots:
                    halo_copy(False, slot - evals).wait_recv()

            for u, slot in enumerate(slots):
                came = slot - evals
                centre = jnp.concatenate(
                    [halo[0, came].astype(jnp.float32), own[came], halo[1, came].astype(jnp.float32)],
                    axis=1,
                )
                spread(u, [
                    pltpu.roll(centre, 1, 1).astype(jnp.bfloat16),
                    centre.astype(jnp.bfloat16),
                    pltpu.roll(centre, low_rows * lanes - 1, 1).astype(jnp.bfloat16),
                ])
        for h0 in range(0, hid_rows, 2):
            n = min(2, hid_rows - h0)
            span = slice(h0 * lanes, (h0 + n) * lanes)
            for u in range(group):
                if k:
                    pre = jnp.dot(win[...], im[u, :, span], preferred_element_type=jnp.float32)
                else:
                    pre = pre0[:, span]
                first_layer(u, pre, times[u], h0, n)
        ready = []
        for s0 in [*range(0, sec_rows, 2), sec_rows]:
            n = min(2, sec_rows - s0)
            fresh = [(u, s0, n, second_layer(u, s0, n)) for u in range(group if n else 0)]
            for u, r0, m, second in ready:
                ysum[u, :, r0 * lanes : (r0 + m) * lanes] = jnp.dot(
                    wout[...], second, preferred_element_type=jnp.float32
                )
            ready = fresh
        for u in range(group):
            state = own[slots[u] - evals] if k else lat[...]
            step = table[times[u], 1:2, :]
            summed = summed + jnp.concatenate([step] * rows, axis=1) * (state + last_layer(u))
            reached = lat[...] + summed
            if k < ITERS - 1:
                reached = reached * flat
                own[slots[u]] = reached
                stage[slots[u]] = reached.astype(jnp.bfloat16)
                if u == 0:
                    @pl.when(j0 == k)
                    def _(summed=summed):
                        start[...] = summed
            else:
                final[times[u]] = reached
        if k < ITERS - 1:
            @pl.when(p > 0)
            def _():
                for slot in slots:
                    halo_copy(True, slot).start()

            @pl.when(p < peers - 1)
            def _():
                for slot in slots:
                    halo_copy(False, slot).start()
        else:
            for j in times:
                deliver(final.at[j], j)
        return summed

    start[...] = jnp.zeros_like(start)
    for k in range(ITERS):

        def body(i, summed, k=k):
            return advance(k, k + i * group, summed)

        lax.fori_loop(0, evals // group, body, start[...])
        if k < ITERS - 1:
            deliver(own.at[k * evals], jnp.int32(k))

    for s in range(1, sections):
        table_copy(s).wait_send()

    @pl.when(p > 0)
    def _():
        first_copy(True).wait_send()

    @pl.when(p < peers - 1)
    def _():
        first_copy(False).wait_send()

    def drain(slot, carry):
        @pl.when(p > 0)
        def _():
            halo_copy(True, slot).wait_send()

        @pl.when(p < peers - 1)
        def _():
            halo_copy(False, slot).wait_send()

        return carry

    lax.fori_loop(0, (ITERS - 1) * evals, drain, 0)

    for j in range(total):
        @pl.when(jnp.int32(j // per) != q)
        def _(j=j):
            final_copy(final.at[j], jnp.int32(j)).wait_send()

    for s in range(sections):
        @pl.when(q != s)
        def _(s=s):
            for j in range(per):
                pltpu.make_async_remote_copy(
                    src_ref=landed.at[s, j], dst_ref=landed.at[s, j],
                    send_sem=fin_send.at[j], recv_sem=fin_recv.at[s, j],
                    device_id=(jnp.int32(s), p), device_id_type=MESH,
                ).wait_recv()

    for s in range(sections):
        for j in range(per):
            block = landed[s, j]
            for r in range(rows):
                out_ref[j, r, :, s * cols : (s + 1) * cols] = block[
                    :, r * lanes + margin : r * lanes + margin + cols
                ]


def shards(latent, step_size, time_embed, conv_in, conv_mid, conv_out):
    sections, peers = lax.axis_size("tm"), lax.axis_size("pix")
    chan, rows, width = latent.shape
    per, feat = time_embed.shape
    total = sections * per
    cols = width // sections
    margin = 3 * ITERS - 1
    lanes = (cols + 2 * margin + LANES - 1) // LANES * LANES
    evals = total - ITERS + 1
    slots = (ITERS - 1) * evals
    group = next(g for g in (GROUP, 2, 1) if evals % g == 0)
    sizes = (sections, peers, per, total, chan, feat, rows, width, cols, margin, lanes, group)
    vmem = pl.BlockSpec(memory_space=pltpu.VMEM)
    f32, bf16 = jnp.float32, jnp.bfloat16
    dma = pltpu.SemaphoreType.DMA
    out = pl.pallas_call(
        functools.partial(kernel, sizes),
        out_shape=jax.ShapeDtypeStruct((per, rows, chan, width), f32),
        in_specs=[pl.BlockSpec(memory_space=pltpu.HBM)] * 6,
        out_specs=vmem,
        scratch_shapes=[
            pltpu.VMEM((feat, 9 * chan), bf16),
            pltpu.VMEM((feat, 9 * feat), bf16),
            pltpu.VMEM((9 * chan, feat), bf16),
            pltpu.VMEM((chan, rows * lanes), f32),
            pltpu.VMEM((3, chan, rows * lanes), bf16),
            pltpu.VMEM((2, 3, chan, 3 * lanes), bf16),
            pltpu.VMEM((group, 9 * chan, (rows + 4) * lanes), bf16),
            pltpu.VMEM((feat, (rows + 4) * lanes), f32),
            pltpu.VMEM((group, 3 * feat, (rows + 4) * lanes), bf16),
            pltpu.VMEM((group, 9 * chan, (rows + 2) * lanes), f32),
            pltpu.VMEM((8, (rows + 4) * lanes), f32),
            pltpu.VMEM((total, 8, feat), f32),
            pltpu.VMEM((total, feat, lanes), f32),
            pltpu.VMEM((slots, chan, rows * lanes), f32),
            pltpu.VMEM((slots, chan, rows * lanes), bf16),
            pltpu.VMEM((2, slots, chan, 3 * lanes), bf16),
            pltpu.VMEM((total, chan, rows * lanes), f32),
            pltpu.VMEM((sections, per, chan, rows * lanes), f32),
            pltpu.VMEM((chan, rows * lanes), f32),
            pltpu.SMEM(step_size.shape, f32),
            pltpu.VMEM(latent.shape, f32),
            pltpu.VMEM(time_embed.shape, f32),
            pltpu.VMEM((3, 3, chan, feat), bf16),
            pltpu.VMEM(conv_mid.shape, bf16),
            pltpu.VMEM(conv_out.shape, bf16),
            dma((6,)),
            dma((2,)), dma((2,)),
            dma((sections - 1,)), dma((sections - 1,)),
            dma((2, slots)), dma((2, slots)),
            dma((total,)), dma((sections, per)),
        ],
        compiler_params=pltpu.CompilerParams(
            collective_id=0, has_side_effects=True, vmem_limit_bytes=60 * 1024 * 1024
        ),
    )(step_size, latent, time_embed, jnp.swapaxes(conv_in, 2, 3), conv_mid, conv_out)
    return jnp.transpose(out, (0, 2, 1, 3))


def solution(mesh):
    in_specs = (P(None, "pix", None), P("tm"), P("tm", None), P(), P(), P())
    out_specs = P("tm", None, "pix", None)
    return jax.shard_map(shards, mesh=mesh, in_specs=in_specs, out_specs=out_specs, check_vma=False)
```

```python
import functools

import jax
import jax.numpy as jnp
from jax import lax
from jax.experimental import pallas as pl
from jax.experimental.pallas import tpu as pltpu
from jax.sharding import PartitionSpec as P

ITERS = 3
GROUP = 3
LANES = 128
MESH = pl.DeviceIdType.MESH


def kernel(
    sizes,
    step_hbm, latent_hbm, te_hbm, cin_hbm, cmid_hbm, cout_hbm,
    out_ref,
    win, wmid, wout, lat, low0, halo0, im, pre0, hid, ysum, mask,
    table, bias, own, stage, halo, final, landed, start,
    step_ref, latent_ref, te_ref, cin_ref, cmid_ref, cout_ref, load_sem,
    sem0_send, sem0_recv, tab_send, tab_recv, halo_send, halo_recv, fin_send, fin_recv,
):
    sections, peers, per, total, chan, feat, rows, width, cols, margin, lanes, group = sizes
    q, p = lax.axis_index("tm"), lax.axis_index("pix")
    evals = total - ITERS + 1
    edge = 3 * lanes
    hid_rows, sec_rows, low_rows = rows + 4, rows + 2, rows + 6

    loads = [
        pltpu.make_async_copy(source, target, load_sem.at[i])
        for i, (source, target) in enumerate([
            (latent_hbm, latent_ref), (te_hbm, te_ref), (step_hbm, step_ref),
            (cin_hbm, cin_ref), (cmid_hbm, cmid_ref), (cout_hbm, cout_ref),
        ])
    ]
    for load in loads:
        load.start()

    barrier = pltpu.get_barrier_semaphore()
    for s in range(1, sections):
        pl.semaphore_signal(barrier, inc=1, device_id=(lax.rem(q + s, sections), p), device_id_type=MESH)

    @pl.when(p > 0)
    def _():
        pl.semaphore_signal(barrier, inc=1, device_id=(q, p - 1), device_id_type=MESH)

    @pl.when(p < peers - 1)
    def _():
        pl.semaphore_signal(barrier, inc=1, device_id=(q, p + 1), device_id_type=MESH)

    for load in loads[:3]:
        load.wait()

    for j in range(per):
        table[q * per + j] = jnp.concatenate(
            [te_ref[j : j + 1, :], jnp.full((7, feat), step_ref[j], jnp.float32)], axis=0
        )

    padded = (width + 2 * margin + LANES - 1) // LANES * LANES
    for r in range(rows):
        line = jnp.concatenate(
            [latent_ref[:, r, :], jnp.zeros((chan, padded - width), jnp.float32)], axis=1
        )
        for b in range(3):
            shift = lax.rem(margin + 1 - b - q * cols + 2 * padded, padded)
            view = pltpu.roll(line, shift, 1)[:, :lanes]
            low0[b, :, r * lanes : (r + 1) * lanes] = view.astype(jnp.bfloat16)
            if b == 1:
                lat[:, r * lanes : (r + 1) * lanes] = view

    @pl.when(p == 0)
    def _():
        halo0[0] = jnp.zeros(halo0.shape[1:], jnp.bfloat16)
        halo[0] = jnp.zeros(halo.shape[1:], jnp.bfloat16)

    @pl.when(p == peers - 1)
    def _():
        halo0[1] = jnp.zeros(halo0.shape[1:], jnp.bfloat16)
        halo[1] = jnp.zeros(halo.shape[1:], jnp.bfloat16)

    def table_copy(s):
        mine = table.at[pl.ds(q * per, per)]
        return pltpu.make_async_remote_copy(
            src_ref=mine, dst_ref=mine, send_sem=tab_send.at[s - 1], recv_sem=tab_recv.at[s - 1],
            device_id=(lax.rem(q + s, sections), p), device_id_type=MESH,
        )

    def first_copy(up):
        src = low0.at[:, :, pl.ds(0 if up else (rows - 3) * lanes, edge)]
        return pltpu.make_async_remote_copy(
            src_ref=src, dst_ref=halo0.at[1 if up else 0],
            send_sem=sem0_send.at[1 if up else 0], recv_sem=sem0_recv.at[1 if up else 0],
            device_id=(q, p - 1 if up else p + 1), device_id_type=MESH,
        )

    def halo_copy(up, slot):
        src = stage.at[slot, :, pl.ds(0 if up else (rows - 3) * lanes, edge)]
        side = 1 if up else 0
        return pltpu.make_async_remote_copy(
            src_ref=src, dst_ref=halo.at[side, slot],
            send_sem=halo_send.at[side, slot], recv_sem=halo_recv.at[side, slot],
            device_id=(q, p - 1 if up else p + 1), device_id_type=MESH,
        )

    def final_copy(source, j):
        return pltpu.make_async_remote_copy(
            src_ref=source, dst_ref=landed.at[q, lax.rem(j, per)],
            send_sem=fin_send.at[j], recv_sem=fin_recv.at[q, lax.rem(j, per)],
            device_id=(lax.div(j, per), p), device_id_type=MESH,
        )

    def deliver(source, j):
        owner = lax.div(jnp.int32(j), jnp.int32(per))

        @pl.when(owner == q)
        def _():
            landed[q, lax.rem(j, per)] = source[...]

        @pl.when(owner != q)
        def _():
            final_copy(source, j).start()

    pl.semaphore_wait(
        barrier, sections - 1 + (p > 0).astype(jnp.int32) + (p < peers - 1).astype(jnp.int32)
    )

    @pl.when(p > 0)
    def _():
        first_copy(True).start()

    @pl.when(p < peers - 1)
    def _():
        first_copy(False).start()

    for s in range(1, sections):
        table_copy(s).start()

    for load in loads[3:]:
        load.wait()

    for a in range(3):
        for b in range(3):
            t = 3 * a + b
            wmid[:, t * feat : (t + 1) * feat] = cmid_ref[a, b]
            wout[t * chan : (t + 1) * chan, :] = cout_ref[a, b]

    taps = jnp.concatenate([cin_ref[t // 3, t % 3] for t in range(9)], axis=0)
    win[...] = taps.astype(jnp.float32).T.astype(jnp.bfloat16)

    col = lax.broadcasted_iota(jnp.int32, (8, lanes), 1) + (q * cols - margin)
    inside = jnp.where((col >= 0) & (col < width), 0.5, 0.0).astype(jnp.float32)
    for h in range(hid_rows):
        row = p * rows - 2 + h
        valid = ((row >= 0) & (row < peers * rows)).astype(jnp.float32)
        mask[:, h * lanes : (h + 1) * lanes] = inside * valid

    def gated(v, m):
        h = v * m
        return h + h * jnp.tanh(h)

    def spread(u, lows):
        for a in range(3):
            for b in range(3):
                t = 3 * a + b
                im[u, t * chan : (t + 1) * chan, :] = lows[b][:, a * lanes : (a + hid_rows) * lanes]

    def first_layer(u, pre, j, h0, count):
        te = bias[j]
        for i in range(count):
            h = h0 + i
            v = pre[:, i * lanes : (i + 1) * lanes] + te
            x = gated(v, mask[0:1, h * lanes : (h + 1) * lanes]).astype(jnp.bfloat16)
            span = slice(h * lanes, (h + 1) * lanes)
            hid[u, 0:feat, span] = pltpu.roll(x, 1, 1)
            hid[u, feat : 2 * feat, span] = x
            hid[u, 2 * feat :, span] = pltpu.roll(x, lanes - 1, 1)

    def second_layer(u, s0, n):
        x = jnp.concatenate(
            [hid[u, :, (s0 + a) * lanes : (s0 + a + n) * lanes] for a in range(3)], axis=0
        )
        v = jnp.dot(wmid[...], x, preferred_element_type=jnp.float32)
        return gated(v, mask[0:1, (s0 + 1) * lanes : (s0 + 1 + n) * lanes]).astype(jnp.bfloat16)

    def last_layer(u):
        parts = []
        for b in range(3):
            z = None
            for a in range(3):
                t = 3 * a + b
                y = ysum[u, t * chan : (t + 1) * chan, a * lanes : (a + rows) * lanes]
                z = y if z is None else z + y
            parts.append(z)
        return parts[1] + pltpu.roll(parts[0], 1, 1) + pltpu.roll(parts[2], rows * lanes - 1, 1)

    @pl.when(p < peers - 1)
    def _():
        first_copy(True).wait_recv()

    @pl.when(p > 0)
    def _():
        first_copy(False).wait_recv()

    spread(0, [jnp.concatenate([halo0[0, b], low0[b], halo0[1, b]], axis=1) for b in range(3)])
    for h0 in range(0, hid_rows, 2):
        n = min(2, hid_rows - h0)
        span = slice(h0 * lanes, (h0 + n) * lanes)
        pre0[:, span] = jnp.dot(win[...], im[0, :, span], preferred_element_type=jnp.float32)

    for s in range(1, sections):
        table_copy(s).wait_recv()
    for j in range(total):
        bias[j] = jnp.broadcast_to(table[j, 0:1, :], (lanes, feat)).T

    flat = jnp.concatenate([inside[0:1, :] * 2.0] * rows, axis=1)

    def advance(k, j0, summed):
        slots = [k * evals + j0 + u - k for u in range(group)]
        times = [j0 + u for u in range(group)]
        if k:
            @pl.when(p < peers - 1)
            def _():
                for slot in slots:
                    halo_copy(True, slot - evals).wait_recv()

            @pl.when(p > 0)
            def _():
                for slot in slots:
                    halo_copy(False, slot - evals).wait_recv()

            for u, slot in enumerate(slots):
                came = slot - evals
                centre = jnp.concatenate(
                    [halo[0, came], stage[came], halo[1, came]],
                    axis=1,
                )
                spread(u, [
                    pltpu.roll(centre, 1, 1),
                    centre,
                    pltpu.roll(centre, low_rows * lanes - 1, 1),
                ])
        for h0 in range(0, hid_rows, 2):
            n = min(2, hid_rows - h0)
            span = slice(h0 * lanes, (h0 + n) * lanes)
            for u in range(group):
                if k:
                    pre = jnp.dot(win[...], im[u, :, span], preferred_element_type=jnp.float32)
                else:
                    pre = pre0[:, span]
                first_layer(u, pre, times[u], h0, n)
        ready = []
        for s0 in [*range(0, sec_rows, 2), sec_rows]:
            n = min(2, sec_rows - s0)
            fresh = [(u, s0, n, second_layer(u, s0, n)) for u in range(group if n else 0)]
            for u, r0, m, second in ready:
                ysum[u, :, r0 * lanes : (r0 + m) * lanes] = jnp.dot(
                    wout[...], second, preferred_element_type=jnp.float32
                )
            ready = fresh
        for u in range(group):
            state = own[slots[u] - evals] if k else lat[...]
            step = table[times[u], 1:2, :]
            summed = summed + jnp.concatenate([step] * rows, axis=1) * (state + last_layer(u))
            reached = lat[...] + summed
            if k < ITERS - 1:
                reached = reached * flat
                own[slots[u]] = reached
                stage[slots[u]] = reached.astype(jnp.bfloat16)
                if u == 0:
                    @pl.when(j0 == k)
                    def _(summed=summed):
                        start[...] = summed
            else:
                final[times[u]] = reached
        if k < ITERS - 1:
            @pl.when(p > 0)
            def _():
                for slot in slots:
                    halo_copy(True, slot).start()

            @pl.when(p < peers - 1)
            def _():
                for slot in slots:
                    halo_copy(False, slot).start()
        else:
            for j in times:
                deliver(final.at[j], j)
        return summed

    start[...] = jnp.zeros_like(start)
    for k in range(ITERS):

        def body(i, summed, k=k):
            return advance(k, k + i * group, summed)

        lax.fori_loop(0, evals // group, body, start[...])
        if k < ITERS - 1:
            deliver(own.at[k * evals], jnp.int32(k))

    for s in range(1, sections):
        table_copy(s).wait_send()

    @pl.when(p > 0)
    def _():
        first_copy(True).wait_send()

    @pl.when(p < peers - 1)
    def _():
        first_copy(False).wait_send()

    def drain(slot, carry):
        @pl.when(p > 0)
        def _():
            halo_copy(True, slot).wait_send()

        @pl.when(p < peers - 1)
        def _():
            halo_copy(False, slot).wait_send()

        return carry

    lax.fori_loop(0, (ITERS - 1) * evals, drain, 0)

    for j in range(total):
        @pl.when(jnp.int32(j // per) != q)
        def _(j=j):
            final_copy(final.at[j], jnp.int32(j)).wait_send()

    for s in range(sections):
        @pl.when(q != s)
        def _(s=s):
            for j in range(per):
                pltpu.make_async_remote_copy(
                    src_ref=landed.at[s, j], dst_ref=landed.at[s, j],
                    send_sem=fin_send.at[j], recv_sem=fin_recv.at[s, j],
                    device_id=(jnp.int32(s), p), device_id_type=MESH,
                ).wait_recv()

    for s in range(sections):
        for j in range(per):
            block = landed[s, j]
            for r in range(rows):
                out_ref[j, r, :, s * cols : (s + 1) * cols] = block[
                    :, r * lanes + margin : r * lanes + margin + cols
                ]


def shards(latent, step_size, time_embed, conv_in, conv_mid, conv_out):
    sections, peers = lax.axis_size("tm"), lax.axis_size("pix")
    chan, rows, width = latent.shape
    per, feat = time_embed.shape
    total = sections * per
    cols = width // sections
    margin = 3 * ITERS - 1
    lanes = (cols + 2 * margin + LANES - 1) // LANES * LANES
    evals = total - ITERS + 1
    slots = (ITERS - 1) * evals
    group = next(g for g in (GROUP, 2, 1) if evals % g == 0)
    sizes = (sections, peers, per, total, chan, feat, rows, width, cols, margin, lanes, group)
    vmem = pl.BlockSpec(memory_space=pltpu.VMEM)
    f32, bf16 = jnp.float32, jnp.bfloat16
    dma = pltpu.SemaphoreType.DMA
    out = pl.pallas_call(
        functools.partial(kernel, sizes),
        out_shape=jax.ShapeDtypeStruct((per, rows, chan, width), f32),
        in_specs=[pl.BlockSpec(memory_space=pltpu.HBM)] * 6,
        out_specs=vmem,
        scratch_shapes=[
            pltpu.VMEM((feat, 9 * chan), bf16),
            pltpu.VMEM((feat, 9 * feat), bf16),
            pltpu.VMEM((9 * chan, feat), bf16),
            pltpu.VMEM((chan, rows * lanes), f32),
            pltpu.VMEM((3, chan, rows * lanes), bf16),
            pltpu.VMEM((2, 3, chan, 3 * lanes), bf16),
            pltpu.VMEM((group, 9 * chan, (rows + 4) * lanes), bf16),
            pltpu.VMEM((feat, (rows + 4) * lanes), f32),
            pltpu.VMEM((group, 3 * feat, (rows + 4) * lanes), bf16),
            pltpu.VMEM((group, 9 * chan, (rows + 2) * lanes), f32),
            pltpu.VMEM((8, (rows + 4) * lanes), f32),
            pltpu.VMEM((total, 8, feat), f32),
            pltpu.VMEM((total, feat, lanes), f32),
            pltpu.VMEM((slots, chan, rows * lanes), f32),
            pltpu.VMEM((slots, chan, rows * lanes), bf16),
            pltpu.VMEM((2, slots, chan, 3 * lanes), bf16),
            pltpu.VMEM((total, chan, rows * lanes), f32),
            pltpu.VMEM((sections, per, chan, rows * lanes), f32),
            pltpu.VMEM((chan, rows * lanes), f32),
            pltpu.SMEM(step_size.shape, f32),
            pltpu.VMEM(latent.shape, f32),
            pltpu.VMEM(time_embed.shape, f32),
            pltpu.VMEM((3, 3, chan, feat), bf16),
            pltpu.VMEM(conv_mid.shape, bf16),
            pltpu.VMEM(conv_out.shape, bf16),
            dma((6,)),
            dma((2,)), dma((2,)),
            dma((sections - 1,)), dma((sections - 1,)),
            dma((2, slots)), dma((2, slots)),
            dma((total,)), dma((sections, per)),
        ],
        compiler_params=pltpu.CompilerParams(
            collective_id=0, has_side_effects=True, vmem_limit_bytes=60 * 1024 * 1024
        ),
    )(step_size, latent, time_embed, jnp.swapaxes(conv_in, 2, 3), conv_mid, conv_out)
    return jnp.transpose(out, (0, 2, 1, 3))


def solution(mesh):
    in_specs = (P(None, "pix", None), P("tm"), P("tm", None), P(), P(), P())
    out_specs = P("tm", None, "pix", None)
    return jax.shard_map(shards, mesh=mesh, in_specs=in_specs, out_specs=out_specs, check_vma=False)
```
